128 devices in a mesh: dp: 8 (over x, core), tensor: 16 (over z, y).
Axes of the slice: x: 4, y: 4, z: 4, core: 2. Of those that a mesh axis runs over, the one named last changes fastest.
Arguments:
- grad_attn: bfloat16 [8, 8192, 4096], P('dp', 'tensor'), may hold values from -6 to 6
- error_attn: bfloat16 [8, 8192, 4096], P('dp', 'tensor'), may hold values from -3 to 3
- q_attn: float32 [16, 4096], replicated, may hold values from -0.09375 to 0.09375
Outputs:
- approx_attn: bfloat16 [8192, 4096], P('tensor', 'dp')
- new_error_attn: bfloat16 [8, 8192, 4096], P('dp', 'tensor')
- new_q_attn: float32 [16, 4096], replicated
The draws below stay inside these ranges and needn't reach their ends.
All inputs are finite; a program needn't handle non-finite values.
Results may differ from the reference program's by a relative error of at most 0.012.
Values sent between devices are 32-bit elements; how exact they have to be, the bound alone decides.
No kernel may reach another device: no remote copies, remote signals or barrier semaphores. Data moves between devices by JAX's collectives and lax.ppermute only.
A program may use at most 64 MiB of HBM per device.

```python
import jax
import jax.numpy as jnp
from jax import lax

COLS = 4096
RANK = 16
ATTN_ROWS = 8192
REPLICAS = 8
N_DP = 8


def level_of(own_key, extent, split, low, largest):
    def one(axis_at, parts):
        steps = jax.random.uniform(jax.random.fold_in(jax.random.fold_in(own_key, 6), axis_at), (parts,), jnp.float32, low / len(split), largest / len(split))
        return jnp.repeat(jnp.exp(steps), extent[axis_at] // parts).reshape((-1,) + (1,) * (len(extent) - axis_at - 1))

    loudness = one(*split[0])
    for cut in split[1:]:
        loudness = loudness * one(*cut)
    return loudness


def centred(stream_key, extent, width, reach, shards=(), kind=jnp.bfloat16):
    drawn = jax.random.normal(stream_key, extent, jnp.float32) * width
    if len(shards) > 0:
        drawn = level_of(stream_key, extent, shards, -0.22, 0.18) * drawn
    return jnp.clip(drawn, min=-reach, max=reach).astype(kind)


def setup_inputs(seed: int = 0) -> dict:
    seeds = jax.random.split(jax.random.key(seed), 4)
    grad_attn = centred(seeds[0], (REPLICAS, ATTN_ROWS, COLS), 1.0, 6.0, ((0, 8), (1, 16)))
    error_attn = centred(seeds[1], (REPLICAS, ATTN_ROWS, COLS), 0.5, 3.0, ((0, 8), (1, 16)))
    q_attn = centred(seeds[2], (RANK, COLS), COLS ** -0.5, 0.09375, (), jnp.float32)
    return {"grad_attn": grad_attn, "error_attn": error_attn, "q_attn": q_attn}


def reference(grad_attn, error_attn, q_attn):
    merged = (grad_attn.astype(jnp.float32) + error_attn.astype(jnp.float32)).astype(jnp.bfloat16)
    factor = q_attn.astype(jnp.bfloat16)
    rows = merged.shape[1]

    def add_left(total, block):
        term = lax.dot_general(block.astype(jnp.float32), factor.astype(jnp.float32), (((1,), (1,)), ((), ())), preferred_element_type=jnp.float32)
        return (total + term, None)
    left, _ = lax.scan(add_left, jnp.zeros((rows, RANK), jnp.float32), merged)
    left = left / N_DP
    gram = jnp.dot(left.T, left, precision=lax.Precision.HIGHEST)
    lower = jnp.linalg.cholesky(gram)
    basis = lax.linalg.triangular_solve(lower, left, left_side=False, lower=True, transpose_a=True)
    basis_b = basis.astype(jnp.bfloat16)

    def add_right(total, block):
        term = lax.dot_general(basis_b.astype(jnp.float32), block.astype(jnp.float32), (((0,), (0,)), ((), ())), preferred_element_type=jnp.float32)
        return (total + term, None)
    right, _ = lax.scan(add_right, jnp.zeros((RANK, merged.shape[2]), jnp.float32), merged)
    right = right / N_DP
    approx = jnp.dot(basis_b.astype(jnp.float32), right.astype(jnp.bfloat16).astype(jnp.float32), preferred_element_type=jnp.float32)
    new_error = (merged.astype(jnp.float32) - approx[None]).astype(jnp.bfloat16)
    return (approx.astype(jnp.bfloat16), new_error, right)
```

```python
import functools

import jax
import jax.numpy as jnp
from jax import lax
from jax.experimental import pallas as pl
from jax.experimental.pallas import tpu as pltpu
from jax.sharding import PartitionSpec as P

F32, BF16 = jnp.float32, jnp.bfloat16
ROWS, COLS, RANK = 512, 4096, 16
LANES = 128
TILES = COLS // LANES
GROUP = 4
GROUPS = RANK // GROUP
LIMIT = 40 * 1024 * 1024


def split3(value):
    high = value.astype(BF16)
    rest = value - high.astype(F32)
    middle = rest.astype(BF16)
    return high, middle, (rest - middle.astype(F32)).astype(BF16)


MERGE_STEPS = 8
MERGE_ROWS = ROWS // MERGE_STEPS


def merge_kernel(grad, error, q, merged, left_t, grad_v, error_v, left_v, sems):
    def copies(i):
        rows = pl.ds(i * MERGE_ROWS, MERGE_ROWS)
        return (
            pltpu.make_async_copy(grad.at[rows], grad_v.at[rows], sems.at[0, i]),
            pltpu.make_async_copy(error.at[rows], error_v.at[rows], sems.at[1, i]),
        )

    for i in range(MERGE_STEPS):
        for copy in copies(i):
            copy.start()
    factor = q[...].astype(BF16)
    for i in range(MERGE_STEPS):
        for copy in copies(i):
            copy.wait()
        rows = pl.ds(i * MERGE_ROWS, MERGE_ROWS)
        block = (grad_v[rows].astype(F32) + error_v[rows].astype(F32)).astype(BF16)
        merged[rows] = block
        left_v[rows] = lax.dot_general(
            block, factor, (((1,), (1,)), ((), ())), preferred_element_type=F32
        )
    left_t[...] = left_v[...].T * 0.125


def merge(grad, error, q):
    return pl.pallas_call(
        merge_kernel,
        out_shape=(
            pltpu.VMEM((ROWS, COLS), BF16),
            pltpu.VMEM((RANK, ROWS), F32),
        ),
        in_specs=[
            pl.BlockSpec(memory_space=pltpu.HBM),
            pl.BlockSpec(memory_space=pltpu.HBM),
            pl.BlockSpec(memory_space=pltpu.VMEM),
        ],
        out_specs=(
            pl.BlockSpec(memory_space=pltpu.VMEM),
            pl.BlockSpec(memory_space=pltpu.VMEM),
        ),
        scratch_shapes=[
            pltpu.VMEM((ROWS, COLS), BF16),
            pltpu.VMEM((ROWS, COLS), BF16),
            pltpu.VMEM((ROWS, RANK), F32),
            pltpu.SemaphoreType.DMA((2, MERGE_STEPS)),
        ],
        compiler_params=pltpu.CompilerParams(vmem_limit_bytes=LIMIT),
        name="merge_left",
    )(grad, error, q)


def right_kernel(own, one, two, three, merged, left_t, parts):
    left = (own[...] + two[...]) + (one[...] + three[...])
    left_t[...] = left
    pieces = jnp.concatenate(split3(left), axis=0)
    for tile in range(0, COLS, 512):
        product = jnp.dot(
            pieces, merged[:, tile : tile + 512], preferred_element_type=F32
        )
        product = (product[2 * RANK :] + product[RANK : 2 * RANK]) + product[:RANK]
        for j in range(4):
            for g in range(GROUPS):
                parts[g * TILES + tile // LANES + j] = product[
                    g * GROUP : (g + 1) * GROUP, j * LANES : (j + 1) * LANES
                ]


def right_product(own, one, two, three, merged):
    return pl.pallas_call(
        right_kernel,
        out_shape=(
            pltpu.VMEM((RANK, ROWS), F32),
            pltpu.VMEM((GROUPS * TILES, GROUP, LANES), F32),
        ),
        in_specs=[pl.BlockSpec(memory_space=pltpu.VMEM)] * 5,
        out_specs=(pl.BlockSpec(memory_space=pltpu.VMEM),) * 2,
        compiler_params=pltpu.CompilerParams(vmem_limit_bytes=LIMIT),
        name="right_parts",
    )(own, one, two, three, merged)


OUT_STEPS = 8
OUT_ROWS = ROWS // OUT_STEPS


def inverse_factor(gram):
    row = lax.broadcasted_iota(jnp.int32, (RANK, RANK), 0)
    col = lax.broadcasted_iota(jnp.int32, (RANK, RANK), 1)
    eye = (row == col).astype(F32)
    work = jnp.concatenate([gram, eye], axis=1)
    rows_at = lax.broadcasted_iota(jnp.int32, (RANK, 1), 0)
    result = jnp.zeros((RANK, 2 * RANK), F32)
    for k in range(RANK):
        pivot_row = work[k : k + 1, :]
        scaled = pivot_row * lax.rsqrt(work[k : k + 1, k : k + 1])
        result = jnp.where(rows_at == k, scaled, result)
        ratio = work[:, k : k + 1] / work[k : k + 1, k : k + 1]
        work = work - jnp.where(rows_at > k, ratio, 0.0) * pivot_row
    return result[:, RANK:]


def finish_kernel(
    place, parts, left_t, q, merged, approx, new_error, right, right_b, error_v, sems
):
    for j in range(TILES):
        for g in range(GROUPS):
            right[g * GROUP : (g + 1) * GROUP, j * LANES : (j + 1) * LANES] = (
                parts[g * TILES + j] * 0.125
            )
    total = right[...]
    factor = q[...].astype(BF16)
    gram = lax.dot_general(
        jnp.concatenate(split3(total), axis=0),
        factor,
        (((1,), (1,)), ((), ())),
        preferred_element_type=F32,
    )
    gram = (gram[2 * RANK :] + gram[RANK : 2 * RANK]) + gram[:RANK]
    inverse = inverse_factor(gram)
    exact = functools.partial(
        jnp.dot, preferred_element_type=F32, precision=lax.Precision.HIGHEST
    )
    total = exact(inverse, total)
    right[...] = total
    right_b[...] = total.astype(BF16)
    basis = exact(inverse, left_t[...]).astype(BF16).T

    def out_copy(i):
        rows = pl.ds(i * OUT_ROWS, OUT_ROWS)
        return pltpu.make_async_copy(error_v.at[rows], new_error.at[rows], sems.at[i])

    columns = pl.ds(pl.multiple_of(place[0] * 512, 512), 512)
    for i in range(OUT_STEPS):
        rows = pl.ds(i * OUT_ROWS, OUT_ROWS)
        block = basis[i * OUT_ROWS : (i + 1) * OUT_ROWS]
        product = jnp.dot(block, right_b[...], preferred_element_type=F32)
        error_v[rows] = (merged[rows].astype(F32) - product).astype(BF16)
        out_copy(i).start()
    approx[...] = jnp.dot(
        basis, right_b[:, columns], preferred_element_type=F32
    ).astype(BF16)
    for i in range(OUT_STEPS):
        out_copy(i).wait()


def finish(place, parts, left_t, q, merged):
    vmem = pl.BlockSpec(memory_space=pltpu.VMEM)
    return pl.pallas_call(
        finish_kernel,
        out_shape=(
            jax.ShapeDtypeStruct((ROWS, 512), BF16),
            jax.ShapeDtypeStruct((ROWS, COLS), BF16),
            jax.ShapeDtypeStruct((RANK, COLS), F32),
        ),
        in_specs=[pl.BlockSpec(memory_space=pltpu.SMEM)] + [vmem] * 4,
        out_specs=(vmem, pl.BlockSpec(memory_space=pltpu.HBM), vmem),
        scratch_shapes=[
            pltpu.VMEM((RANK, COLS), BF16),
            pltpu.VMEM((ROWS, COLS), BF16),
            pltpu.SemaphoreType.DMA((OUT_STEPS,)),
        ],
        compiler_params=pltpu.CompilerParams(vmem_limit_bytes=LIMIT),
        name="finish",
    )(place, parts, left_t, q, merged)


def local(grad_attn, error_attn, q_attn):
    merged, left_t = merge(grad_attn[0], error_attn[0], q_attn)

    def moved(value, pairs):
        return lax.ppermute(value, "dp", pairs)

    pair = left_t + moved(left_t, [(i, i ^ 1) for i in range(8)])
    others = [moved(pair, [(i, (i + 2 * k) % 8) for i in range(8)]) for k in (1, 2, 3)]
    left_t, parts = right_product(pair, *others, merged)
    parts = lax.all_to_all(parts, ("dp", "tensor"), 0, 0, tiled=True)
    chunk = jnp.sum(parts, axis=0, keepdims=True)
    parts = jnp.broadcast_to(chunk, parts.shape)
    parts = lax.all_to_all(parts, ("dp", "tensor"), 0, 0, tiled=True)
    place = lax.axis_index("dp").reshape(1).astype(jnp.int32)
    approx, new_error, right = finish(place, parts, left_t, q_attn, merged)
    return (approx, new_error[None], right)


def solution(mesh):
    placed = (P("dp", "tensor", None), P("dp", "tensor", None), P())
    return jax.shard_map(
        local,
        mesh=mesh,
        in_specs=placed,
        out_specs=(P("tensor", "dp"), P("dp", "tensor", None), P()),
        check_vma=False,
    )
```

```python
import functools

import jax
import jax.numpy as jnp
from jax import lax
from jax.experimental import pallas as pl
from jax.experimental.pallas import tpu as pltpu
from jax.sharding import PartitionSpec as P

F32, BF16 = jnp.float32, jnp.bfloat16
ROWS, COLS, RANK = 512, 4096, 16
LANES = 128
TILES = COLS // LANES
GROUP = 4
GROUPS = RANK // GROUP
LIMIT = 40 * 1024 * 1024


def split3(value):
    high = value.astype(BF16)
    rest = value - high.astype(F32)
    middle = rest.astype(BF16)
    return high, middle, (rest - middle.astype(F32)).astype(BF16)


MERGE_STEPS = 8
MERGE_ROWS = ROWS // MERGE_STEPS


def merge_kernel(grad, error, q, merged, left_t, grad_v, error_v, left_v, sems):
    def copies(i):
        rows = pl.ds(i * MERGE_ROWS, MERGE_ROWS)
        return (
            pltpu.make_async_copy(grad.at[rows], grad_v.at[rows], sems.at[0, i]),
            pltpu.make_async_copy(error.at[rows], error_v.at[rows], sems.at[1, i]),
        )

    for i in range(MERGE_STEPS):
        for copy in copies(i):
            copy.start()
    factor = q[...].astype(BF16)
    for i in range(MERGE_STEPS):
        for copy in copies(i):
            copy.wait()
        rows = pl.ds(i * MERGE_ROWS, MERGE_ROWS)
        block = (grad_v[rows].astype(F32) + error_v[rows].astype(F32)).astype(BF16)
        merged[rows] = block
        left_v[rows] = lax.dot_general(
            block, factor, (((1,), (1,)), ((), ())), preferred_element_type=F32
        )
    left_t[...] = left_v[...].T * 0.125


def merge(grad, error, q):
    return pl.pallas_call(
        merge_kernel,
        out_shape=(
            pltpu.VMEM((ROWS, COLS), BF16),
            pltpu.VMEM((RANK, ROWS), F32),
        ),
        in_specs=[
            pl.BlockSpec(memory_space=pltpu.HBM),
            pl.BlockSpec(memory_space=pltpu.HBM),
            pl.BlockSpec(memory_space=pltpu.VMEM),
        ],
        out_specs=(
            pl.BlockSpec(memory_space=pltpu.VMEM),
            pl.BlockSpec(memory_space=pltpu.VMEM),
        ),
        scratch_shapes=[
            pltpu.VMEM((ROWS, COLS), BF16),
            pltpu.VMEM((ROWS, COLS), BF16),
            pltpu.VMEM((ROWS, RANK), F32),
            pltpu.SemaphoreType.DMA((2, MERGE_STEPS)),
        ],
        compiler_params=pltpu.CompilerParams(vmem_limit_bytes=LIMIT),
        name="merge_left",
    )(
        pltpu.with_memory_space_constraint(grad, pltpu.HBM),
        pltpu.with_memory_space_constraint(error, pltpu.HBM),
        q,
    )


def right_kernel(own, one, two, three, merged, left_t, parts):
    left = (own[...] + two[...]) + (one[...] + three[...])
    left_t[...] = left
    pieces = jnp.concatenate(split3(left), axis=0)
    for tile in range(0, COLS, 512):
        product = jnp.dot(
            pieces, merged[:, tile : tile + 512], preferred_element_type=F32
        )
        product = (product[2 * RANK :] + product[RANK : 2 * RANK]) + product[:RANK]
        for j in range(4):
            for g in range(GROUPS):
                parts[g * TILES + tile // LANES + j] = product[
                    g * GROUP : (g + 1) * GROUP, j * LANES : (j + 1) * LANES
                ]


def right_product(own, one, two, three, merged):
    return pl.pallas_call(
        right_kernel,
        out_shape=(
            pltpu.VMEM((RANK, ROWS), F32),
            pltpu.VMEM((GROUPS * TILES, GROUP, LANES), F32),
        ),
        in_specs=[pl.BlockSpec(memory_space=pltpu.VMEM)] * 5,
        out_specs=(pl.BlockSpec(memory_space=pltpu.VMEM),) * 2,
        compiler_params=pltpu.CompilerParams(vmem_limit_bytes=LIMIT),
        name="right_parts",
    )(own, one, two, three, pltpu.with_memory_space_constraint(merged, pltpu.VMEM))


def sum_kernel(parts, chunks):
    total = jnp.sum(parts[...], axis=0, keepdims=True)
    chunks[...] = jnp.broadcast_to(total, chunks.shape)


def sum_parts(parts):
    return pl.pallas_call(
        sum_kernel,
        out_shape=pltpu.VMEM(parts.shape, F32),
        in_specs=[pl.BlockSpec(memory_space=pltpu.VMEM)],
        out_specs=pl.BlockSpec(memory_space=pltpu.VMEM),
        compiler_params=pltpu.CompilerParams(vmem_limit_bytes=LIMIT),
        name="sum_parts",
    )(pltpu.with_memory_space_constraint(parts, pltpu.VMEM))


OUT_STEPS = 8
OUT_ROWS = ROWS // OUT_STEPS


def inverse_factor(gram):
    row = lax.broadcasted_iota(jnp.int32, (RANK, RANK), 0)
    col = lax.broadcasted_iota(jnp.int32, (RANK, RANK), 1)
    eye = (row == col).astype(F32)
    work = jnp.concatenate([gram, eye], axis=1)
    rows_at = lax.broadcasted_iota(jnp.int32, (RANK, 1), 0)
    result = jnp.zeros((RANK, 2 * RANK), F32)
    for k in range(RANK):
        pivot_row = work[k : k + 1, :]
        scaled = pivot_row * lax.rsqrt(work[k : k + 1, k : k + 1])
        result = jnp.where(rows_at == k, scaled, result)
        ratio = work[:, k : k + 1] / work[k : k + 1, k : k + 1]
        work = work - jnp.where(rows_at > k, ratio, 0.0) * pivot_row
    return result[:, RANK:]


def finish_kernel(
    parts, left_t, q, merged, approx, new_error, right, right_b, error_v, sems
):
    for j in range(TILES):
        for g in range(GROUPS):
            right[g * GROUP : (g + 1) * GROUP, j * LANES : (j + 1) * LANES] = (
                parts[g * TILES + j] * 0.125
            )
    total = right[...]
    factor = q[...].astype(BF16)
    gram = lax.dot_general(
        jnp.concatenate(split3(total), axis=0),
        factor,
        (((1,), (1,)), ((), ())),
        preferred_element_type=F32,
    )
    gram = (gram[2 * RANK :] + gram[RANK : 2 * RANK]) + gram[:RANK]
    inverse = inverse_factor(gram)
    exact = functools.partial(
        jnp.dot, preferred_element_type=F32, precision=lax.Precision.HIGHEST
    )
    total = exact(inverse, total)
    right[...] = total
    right_b[...] = total.astype(BF16)
    basis = exact(inverse, left_t[...]).astype(BF16).T

    def out_copy(i):
        rows = pl.ds(i * OUT_ROWS, OUT_ROWS)
        return pltpu.make_async_copy(error_v.at[rows], new_error.at[rows], sems.at[i])

    columns = pl.ds(pl.multiple_of(lax.axis_index("dp") * 512, 512), 512)
    for i in range(OUT_STEPS):
        rows = pl.ds(i * OUT_ROWS, OUT_ROWS)
        block = basis[i * OUT_ROWS : (i + 1) * OUT_ROWS]
        product = jnp.dot(block, right_b[...], preferred_element_type=F32)
        error_v[rows] = (merged[rows].astype(F32) - product).astype(BF16)
        out_copy(i).start()
    approx[...] = jnp.dot(
        basis, right_b[:, columns], preferred_element_type=F32
    ).astype(BF16)
    for i in range(OUT_STEPS):
        out_copy(i).wait()


def finish(parts, left_t, q, merged):
    vmem = pl.BlockSpec(memory_space=pltpu.VMEM)
    return pl.pallas_call(
        finish_kernel,
        out_shape=(
            jax.ShapeDtypeStruct((ROWS, 512), BF16),
            jax.ShapeDtypeStruct((ROWS, COLS), BF16),
            jax.ShapeDtypeStruct((RANK, COLS), F32),
        ),
        in_specs=[vmem] * 4,
        out_specs=(vmem, pl.BlockSpec(memory_space=pltpu.HBM), vmem),
        scratch_shapes=[
            pltpu.VMEM((RANK, COLS), BF16),
            pltpu.VMEM((ROWS, COLS), BF16),
            pltpu.SemaphoreType.DMA((OUT_STEPS,)),
        ],
        compiler_params=pltpu.CompilerParams(vmem_limit_bytes=LIMIT),
        name="finish",
    )(parts, left_t, q, pltpu.with_memory_space_constraint(merged, pltpu.VMEM))


def local(grad_attn, error_attn, q_attn):
    merged, left_t = merge(grad_attn[0], error_attn[0], q_attn)

    def moved(value, pairs):
        return lax.ppermute(value, "dp", pairs)

    pair = left_t + moved(left_t, [(i, i ^ 1) for i in range(8)])
    others = [moved(pair, [(i, (i + 2 * k) % 8) for i in range(8)]) for k in (1, 2, 3)]
    left_t, parts = right_product(pair, *others, merged)
    parts = lax.all_to_all(parts, ("dp", "tensor"), 0, 0, tiled=True)
    parts = sum_parts(parts)
    parts = lax.all_to_all(parts, ("dp", "tensor"), 0, 0, tiled=True)
    approx, new_error, right = finish(parts, left_t, q_attn, merged)
    return (approx, new_error[None], right)


def solution(mesh):
    placed = (P("dp", "tensor", None), P("dp", "tensor", None), P())
    return jax.shard_map(
        local,
        mesh=mesh,
        in_specs=placed,
        out_specs=(P("tensor", "dp"), P("dp", "tensor", None), P()),
        check_vma=False,
    )
```

```python
import functools

import jax
import jax.numpy as jnp
from jax import lax
from jax.experimental import pallas as pl
from jax.experimental.pallas import tpu as pltpu
from jax.sharding import PartitionSpec as P

F32, BF16 = jnp.float32, jnp.bfloat16
ROWS, COLS, RANK = 512, 4096, 16
LANES = 128
TILES = COLS // LANES
GROUP = 4
GROUPS = RANK // GROUP
LIMIT = 40 * 1024 * 1024


def split3(value):
    high = value.astype(BF16)
    rest = value - high.astype(F32)
    middle = rest.astype(BF16)
    return high, middle, (rest - middle.astype(F32)).astype(BF16)


BLOCKS = ((0, 1024), (1024, 1024), (2048, 1024), (3072, 512), (3584, 256), (3840, 256))


def merge_kernel(
    grad, error, q, merged, left_t, factor, grad_v, error_v, q_v, sems, q_sem
):
    def copies(i):
        start, width = BLOCKS[i]
        columns = pl.ds(start, width)
        return (
            pltpu.make_async_copy(
                grad.at[:, columns], grad_v.at[:, columns], sems.at[0, i]
            ),
            pltpu.make_async_copy(
                error.at[:, columns], error_v.at[:, columns], sems.at[1, i]
            ),
        )

    q_copy = pltpu.make_async_copy(q, q_v, q_sem)
    q_copy.start()
    for copy in copies(0):
        copy.start()
    q_copy.wait()
    for i in range(1, len(BLOCKS)):
        for copy in copies(i):
            copy.start()
    factor[...] = q_v[...].astype(BF16)
    left = None
    for i, (start, width) in enumerate(BLOCKS):
        for copy in copies(i):
            copy.wait()
        columns = pl.ds(start, width)
        block = (grad_v[:, columns].astype(F32) + error_v[:, columns].astype(F32)).astype(BF16)
        merged[:, columns] = block
        term = lax.dot_general(
            factor[:, columns],
            block,
            (((1,), (1,)), ((), ())),
            preferred_element_type=F32,
        )
        left = term if left is None else left + term
    left_t[...] = left * 0.125


def merge(grad, error, q):
    hbm = pl.BlockSpec(memory_space=pltpu.HBM)
    vmem = pl.BlockSpec(memory_space=pltpu.VMEM)
    return pl.pallas_call(
        merge_kernel,
        out_shape=(
            pltpu.VMEM((ROWS, COLS), BF16),
            pltpu.VMEM((RANK, ROWS), F32),
            pltpu.VMEM((RANK, COLS), BF16),
        ),
        in_specs=[hbm] * 3,
        out_specs=(vmem, vmem, vmem),
        scratch_shapes=[
            pltpu.VMEM((ROWS, COLS), BF16),
            pltpu.VMEM((ROWS, COLS), BF16),
            pltpu.VMEM((RANK, COLS), F32),
            pltpu.SemaphoreType.DMA((2, len(BLOCKS))),
            pltpu.SemaphoreType.DMA,
        ],
        compiler_params=pltpu.CompilerParams(vmem_limit_bytes=LIMIT),
        name="merge_left",
    )(*(pltpu.with_memory_space_constraint(x, pltpu.HBM) for x in (grad, error, q)))


def right_kernel(own, one, two, three, merged, left_t, parts):
    left = (own[...] + one[...]) + (two[...] + three[...])
    left_t[...] = left
    pieces = jnp.concatenate(split3(left), axis=0)
    for tile in range(0, COLS, 512):
        product = jnp.dot(
            pieces, merged[:, tile : tile + 512], preferred_element_type=F32
        )
        product = (product[2 * RANK :] + product[RANK : 2 * RANK]) + product[:RANK]
        for j in range(4):
            for g in range(GROUPS):
                parts[g * TILES + tile // LANES + j] = product[
                    g * GROUP : (g + 1) * GROUP, j * LANES : (j + 1) * LANES
                ]


def right_product(own, one, two, three, merged):
    return pl.pallas_call(
        right_kernel,
        out_shape=(
            pltpu.VMEM((RANK, ROWS), F32),
            pltpu.VMEM((GROUPS * TILES, GROUP, LANES), F32),
        ),
        in_specs=[pl.BlockSpec(memory_space=pltpu.VMEM)] * 5,
        out_specs=(pl.BlockSpec(memory_space=pltpu.VMEM),) * 2,
        compiler_params=pltpu.CompilerParams(vmem_limit_bytes=LIMIT),
        name="right_parts",
    )(own, one, two, three, pltpu.with_memory_space_constraint(merged, pltpu.VMEM))


def sum_kernel(parts, chunks):
    total = jnp.sum(parts[...], axis=0, keepdims=True)
    chunks[...] = jnp.broadcast_to(total, chunks.shape)


def sum_parts(parts):
    return pl.pallas_call(
        sum_kernel,
        out_shape=pltpu.VMEM(parts.shape, F32),
        in_specs=[pl.BlockSpec(memory_space=pltpu.VMEM)],
        out_specs=pl.BlockSpec(memory_space=pltpu.VMEM),
        compiler_params=pltpu.CompilerParams(vmem_limit_bytes=LIMIT),
        name="sum_parts",
    )(pltpu.with_memory_space_constraint(parts, pltpu.VMEM))


OWN = COLS // 8
OUT_STEPS = COLS // OWN


def inverse_factor(gram):
    row = lax.broadcasted_iota(jnp.int32, (RANK, RANK), 0)
    col = lax.broadcasted_iota(jnp.int32, (RANK, RANK), 1)
    eye = (row == col).astype(F32)
    work = jnp.concatenate([gram, eye], axis=1)
    rows_at = lax.broadcasted_iota(jnp.int32, (RANK, 1), 0)
    result = jnp.zeros((RANK, 2 * RANK), F32)
    for k in range(RANK):
        pivot_row = work[k : k + 1, :]
        scaled = pivot_row * lax.rsqrt(work[k : k + 1, k : k + 1])
        result = jnp.where(rows_at == k, scaled, result)
        ratio = work[:, k : k + 1] / work[k : k + 1, k : k + 1]
        work = work - jnp.where(rows_at > k, ratio, 0.0) * pivot_row
    return result[:, RANK:]


def stacked(left, right):
    a, b, c = split3(left)
    x, y, z = split3(right)
    return (
        jnp.concatenate([c, b, a, b, a, a], axis=1),
        jnp.concatenate([x, y, z, x, y, x], axis=0),
    )


def finish_kernel(
    parts, left_t, factor, merged, approx, new_error, right,
    total_v, right_v, approx_v, error_v, sems, approx_sem, right_sem,
):
    for j in range(TILES):
        for g in range(GROUPS):
            total_v[g * GROUP : (g + 1) * GROUP, j * LANES : (j + 1) * LANES] = (
                parts[g * TILES + j] * 0.125
            )
    gram = lax.dot_general(
        jnp.concatenate(split3(total_v[...]), axis=0),
        factor[...],
        (((1,), (1,)), ((), ())),
        preferred_element_type=F32,
    )
    gram = (gram[2 * RANK :] + gram[RANK : 2 * RANK]) + gram[:RANK]
    inverse = inverse_factor(gram)
    lhs, rhs = stacked(inverse, left_t[...])
    basis = jnp.dot(lhs, rhs, preferred_element_type=F32).astype(BF16).T
    place = lax.axis_index("dp")

    def error_copy(step):
        columns = pl.ds(pl.multiple_of(lax.rem(place + step, OUT_STEPS) * OWN, OWN), OWN)
        return pltpu.make_async_copy(
            error_v.at[:, columns], new_error.at[:, columns], sems.at[step]
        )

    approx_copy = pltpu.make_async_copy(approx_v, approx, approx_sem)
    right_copy = pltpu.make_async_copy(right_v, right, right_sem)
    for step in range(OUT_STEPS):
        columns = pl.ds(pl.multiple_of(lax.rem(place + step, OUT_STEPS) * OWN, OWN), OWN)
        lhs, rhs = stacked(inverse, total_v[:, columns])
        block = jnp.dot(lhs, rhs, preferred_element_type=F32)
        right_v[:, columns] = block
        product = jnp.dot(basis, block.astype(BF16), preferred_element_type=F32)
        error_v[:, columns] = (merged[:, columns].astype(F32) - product).astype(BF16)
        error_copy(step).start()
        if step == 0:
            approx_v[...] = product.astype(BF16)
            approx_copy.start()
    right_copy.start()
    for step in range(OUT_STEPS):
        error_copy(step).wait()
    approx_copy.wait()
    right_copy.wait()


def finish(parts, left_t, factor, merged):
    vmem = pl.BlockSpec(memory_space=pltpu.VMEM)
    hbm = pl.BlockSpec(memory_space=pltpu.HBM)
    return pl.pallas_call(
        finish_kernel,
        out_shape=(
            jax.ShapeDtypeStruct((ROWS, OWN), BF16),
            jax.ShapeDtypeStruct((ROWS, COLS), BF16),
            jax.ShapeDtypeStruct((RANK, COLS), F32),
        ),
        in_specs=[vmem] * 4,
        out_specs=(hbm, hbm, hbm),
        scratch_shapes=[
            pltpu.VMEM((RANK, COLS), F32),
            pltpu.VMEM((RANK, COLS), F32),
            pltpu.VMEM((ROWS, OWN), BF16),
            pltpu.VMEM((ROWS, COLS), BF16),
            pltpu.SemaphoreType.DMA((OUT_STEPS,)),
            pltpu.SemaphoreType.DMA,
            pltpu.SemaphoreType.DMA,
        ],
        compiler_params=pltpu.CompilerParams(vmem_limit_bytes=LIMIT),
        name="finish",
    )(parts, left_t, factor, pltpu.with_memory_space_constraint(merged, pltpu.VMEM))


def local(grad_attn, error_attn, q_attn):
    merged, left_t, factor = merge(grad_attn[0], error_attn[0], q_attn)

    def moved(value, pairs):
        return lax.ppermute(value, "dp", pairs)

    pair = left_t + moved(left_t, [(i, i ^ 1) for i in range(8)])
    others = [moved(pair, [(i, i ^ (2 * k)) for i in range(8)]) for k in (1, 2, 3)]
    left_t, parts = right_product(pair, *others, merged)
    parts = lax.all_to_all(parts, ("dp", "tensor"), 0, 0, tiled=True)
    parts = sum_parts(parts)
    parts = lax.all_to_all(parts, ("dp", "tensor"), 0, 0, tiled=True)
    approx, new_error, right = finish(parts, left_t, factor, merged)
    return (approx, new_error[None], right)


def solution(mesh):
    placed = (P("dp", "tensor", None), P("dp", "tensor", None), P())
    return jax.shard_map(
        local,
        mesh=mesh,
        in_specs=placed,
        out_specs=(P("tensor", "dp"), P("dp", "tensor", None), P()),
        check_vma=False,
    )
```

```python
import functools

import jax
import jax.numpy as jnp
from jax import lax
from jax.experimental import pallas as pl
from jax.experimental.pallas import tpu as pltpu
from jax.sharding import PartitionSpec as P

F32, BF16 = jnp.float32, jnp.bfloat16
ROWS, COLS, RANK = 512, 4096, 16
LANES = 128
TILES = COLS // LANES
GROUP = 4
GROUPS = RANK // GROUP
LIMIT = 40 * 1024 * 1024


def split3(value):
    high = value.astype(BF16)
    rest = value - high.astype(F32)
    middle = rest.astype(BF16)
    return high, middle, (rest - middle.astype(F32)).astype(BF16)


BLOCKS = ((0, 1024), (1024, 1024), (2048, 1024), (3072, 512), (3584, 256), (3840, 256))


def merge_kernel(
    grad, error, q, merged, left_t, factor, grad_v, error_v, q_v, sems, q_sem
):
    def copies(i):
        start, width = BLOCKS[i]
        columns = pl.ds(start, width)
        return (
            pltpu.make_async_copy(
                grad.at[:, columns], grad_v.at[:, columns], sems.at[0, i]
            ),
            pltpu.make_async_copy(
                error.at[:, columns], error_v.at[:, columns], sems.at[1, i]
            ),
        )

    q_copy = pltpu.make_async_copy(q, q_v, q_sem)
    q_copy.start()
    for copy in copies(0):
        copy.start()
    q_copy.wait()
    for i in range(1, len(BLOCKS)):
        for copy in copies(i):
            copy.start()
    factor[...] = q_v[...].astype(BF16)
    left = None
    for i, (start, width) in enumerate(BLOCKS):
        for copy in copies(i):
            copy.wait()
        columns = pl.ds(start, width)
        block = (grad_v[:, columns].astype(F32) + error_v[:, columns].astype(F32)).astype(BF16)
        merged[:, columns] = block
        term = lax.dot_general(
            factor[:, columns],
            block,
            (((1,), (1,)), ((), ())),
            preferred_element_type=F32,
        )
        left = term if left is None else left + term
    left_t[...] = left * 0.125


def merge(grad, error, q):
    hbm = pl.BlockSpec(memory_space=pltpu.HBM)
    vmem = pl.BlockSpec(memory_space=pltpu.VMEM)
    return pl.pallas_call(
        merge_kernel,
        out_shape=(
            pltpu.VMEM((ROWS, COLS), BF16),
            pltpu.VMEM((RANK, ROWS), F32),
            pltpu.VMEM((RANK, COLS), BF16),
        ),
        in_specs=[hbm] * 3,
        out_specs=(vmem, vmem, vmem),
        scratch_shapes=[
            pltpu.VMEM((ROWS, COLS), BF16),
            pltpu.VMEM((ROWS, COLS), BF16),
            pltpu.VMEM((RANK, COLS), F32),
            pltpu.SemaphoreType.DMA((2, len(BLOCKS))),
            pltpu.SemaphoreType.DMA,
        ],
        compiler_params=pltpu.CompilerParams(vmem_limit_bytes=LIMIT),
        name="merge_left",
    )(*(pltpu.with_memory_space_constraint(x, pltpu.HBM) for x in (grad, error, q)))


def right_kernel(own, one, two, three, merged, left_t, parts):
    left = (own[...] + one[...]) + (two[...] + three[...])
    left_t[...] = left
    pieces = jnp.concatenate(split3(left), axis=0)
    for tile in range(0, COLS, 512):
        product = jnp.dot(
            pieces, merged[:, tile : tile + 512], preferred_element_type=F32
        )
        product = (product[2 * RANK :] + product[RANK : 2 * RANK]) + product[:RANK]
        for j in range(4):
            for g in range(GROUPS):
                parts[g * TILES + tile // LANES + j] = product[
                    g * GROUP : (g + 1) * GROUP, j * LANES : (j + 1) * LANES
                ]


def right_product(own, one, two, three, merged):
    return pl.pallas_call(
        right_kernel,
        out_shape=(
            pltpu.VMEM((RANK, ROWS), F32),
            pltpu.VMEM((GROUPS * TILES, GROUP, LANES), F32),
        ),
        in_specs=[pl.BlockSpec(memory_space=pltpu.VMEM)] * 5,
        out_specs=(pl.BlockSpec(memory_space=pltpu.VMEM),) * 2,
        compiler_params=pltpu.CompilerParams(vmem_limit_bytes=LIMIT),
        name="right_parts",
    )(own, one, two, three, pltpu.with_memory_space_constraint(merged, pltpu.VMEM))


def sum_kernel(parts, chunks):
    total = jnp.sum(parts[...], axis=0, keepdims=True)
    chunks[...] = jnp.broadcast_to(total, chunks.shape)


def sum_parts(parts):
    return pl.pallas_call(
        sum_kernel,
        out_shape=pltpu.VMEM(parts.shape, F32),
        in_specs=[pl.BlockSpec(memory_space=pltpu.VMEM)],
        out_specs=pl.BlockSpec(memory_space=pltpu.VMEM),
        compiler_params=pltpu.CompilerParams(vmem_limit_bytes=LIMIT),
        name="sum_parts",
    )(pltpu.with_memory_space_constraint(parts, pltpu.VMEM))


OWN = COLS // 8
OUT_STEPS = COLS // OWN


def inverse_factor(gram):
    width = 2 * RANK
    row = lax.broadcasted_iota(jnp.int32, (RANK, RANK), 0)
    col = lax.broadcasted_iota(jnp.int32, (RANK, RANK), 1)
    work = jnp.concatenate([gram, (row == col).astype(F32)], axis=1)
    rows_at = lax.broadcasted_iota(jnp.int32, (RANK, width), 0)
    columns = [jnp.broadcast_to(gram[:, k : k + 1], (RANK, width)) for k in range(RANK)]
    result = jnp.zeros((RANK, width), F32)
    for k in range(RANK):
        pivot = jnp.broadcast_to(columns[k][k : k + 1], (RANK, width))
        pivot_row = jnp.broadcast_to(work[k : k + 1], (RANK, width))
        result = jnp.where(rows_at == k, pivot_row * lax.rsqrt(pivot), result)
        ratio = jnp.where(rows_at > k, columns[k], 0.0) / pivot
        work = work - ratio * pivot_row
        for j in range(k + 1, RANK):
            columns[j] = columns[j] - ratio * columns[j][k : k + 1]
    return result[:, RANK:]


def stacked(left, right):
    a, b, c = split3(left)
    x, y, z = split3(right)
    return (
        jnp.concatenate([c, b, a, b, a, a], axis=1),
        jnp.concatenate([x, y, z, x, y, x], axis=0),
    )


def finish_kernel(
    parts, left_t, factor, merged, approx, new_error, right,
    total_v, right_v, approx_v, error_v, sems, approx_sem, right_sem,
):
    for j in range(TILES):
        for g in range(GROUPS):
            total_v[g * GROUP : (g + 1) * GROUP, j * LANES : (j + 1) * LANES] = (
                parts[g * TILES + j] * 0.125
            )
    gram = lax.dot_general(
        jnp.concatenate(split3(total_v[...]), axis=0),
        factor[...],
        (((1,), (1,)), ((), ())),
        preferred_element_type=F32,
    )
    gram = (gram[2 * RANK :] + gram[RANK : 2 * RANK]) + gram[:RANK]
    inverse = inverse_factor(gram)
    lhs, rhs = stacked(inverse, left_t[...])
    basis = jnp.dot(lhs, rhs, preferred_element_type=F32).astype(BF16).T
    place = lax.axis_index("dp")

    def error_copy(step):
        columns = pl.ds(pl.multiple_of(lax.rem(place + step, OUT_STEPS) * OWN, OWN), OWN)
        return pltpu.make_async_copy(
            error_v.at[:, columns], new_error.at[:, columns], sems.at[step]
        )

    approx_copy = pltpu.make_async_copy(approx_v, approx, approx_sem)
    right_copy = pltpu.make_async_copy(right_v, right, right_sem)
    for step in range(OUT_STEPS):
        columns = pl.ds(pl.multiple_of(lax.rem(place + step, OUT_STEPS) * OWN, OWN), OWN)
        lhs, rhs = stacked(inverse, total_v[:, columns])
        block = jnp.dot(lhs, rhs, preferred_element_type=F32)
        right_v[:, columns] = block
        product = jnp.dot(basis, block.astype(BF16), preferred_element_type=F32)
        error_v[:, columns] = (merged[:, columns].astype(F32) - product).astype(BF16)
        error_copy(step).start()
        if step == 0:
            approx_v[...] = product.astype(BF16)
            approx_copy.start()
    right_copy.start()
    for step in range(OUT_STEPS):
        error_copy(step).wait()
    approx_copy.wait()
    right_copy.wait()


def finish(parts, left_t, factor, merged):
    vmem = pl.BlockSpec(memory_space=pltpu.VMEM)
    hbm = pl.BlockSpec(memory_space=pltpu.HBM)
    return pl.pallas_call(
        finish_kernel,
        out_shape=(
            jax.ShapeDtypeStruct((ROWS, OWN), BF16),
            jax.ShapeDtypeStruct((ROWS, COLS), BF16),
            jax.ShapeDtypeStruct((RANK, COLS), F32),
        ),
        in_specs=[vmem] * 4,
        out_specs=(hbm, hbm, hbm),
        scratch_shapes=[
            pltpu.VMEM((RANK, COLS), F32),
            pltpu.VMEM((RANK, COLS), F32),
            pltpu.VMEM((ROWS, OWN), BF16),
            pltpu.VMEM((ROWS, COLS), BF16),
            pltpu.SemaphoreType.DMA((OUT_STEPS,)),
            pltpu.SemaphoreType.DMA,
            pltpu.SemaphoreType.DMA,
        ],
        compiler_params=pltpu.CompilerParams(vmem_limit_bytes=LIMIT),
        name="finish",
    )(parts, left_t, factor, pltpu.with_memory_space_constraint(merged, pltpu.VMEM))


def local(grad_attn, error_attn, q_attn):
    merged, left_t, factor = merge(grad_attn[0], error_attn[0], q_attn)

    def moved(value, pairs):
        return lax.ppermute(value, "dp", pairs)

    pair = left_t + moved(left_t, [(i, i ^ 1) for i in range(8)])
    others = [moved(pair, [(i, i ^ (2 * k)) for i in range(8)]) for k in (1, 2, 3)]
    left_t, parts = right_product(pair, *others, merged)
    parts = lax.all_to_all(parts, ("dp", "tensor"), 0, 0, tiled=True)
    parts = sum_parts(parts)
    parts = lax.all_to_all(parts, ("dp", "tensor"), 0, 0, tiled=True)
    approx, new_error, right = finish(parts, left_t, factor, merged)
    return (approx, new_error[None], right)


def solution(mesh):
    placed = (P("dp", "tensor", None), P("dp", "tensor", None), P())
    return jax.shard_map(
        local,
        mesh=mesh,
        in_specs=placed,
        out_specs=(P("tensor", "dp"), P("dp", "tensor", None), P()),
        check_vma=False,
    )
```

```python
import functools

import jax
import jax.numpy as jnp
from jax import lax
from jax.experimental import pallas as pl
from jax.experimental.pallas import tpu as pltpu
from jax.sharding import PartitionSpec as P

F32, BF16 = jnp.float32, jnp.bfloat16
ROWS, COLS, RANK = 512, 4096, 16
LANES = 128
TILES = COLS // LANES
GROUP = 4
GROUPS = RANK // GROUP
LIMIT = 40 * 1024 * 1024


def split3(value):
    high = value.astype(BF16)
    rest = value - high.astype(F32)
    middle = rest.astype(BF16)
    return high, middle, (rest - middle.astype(F32)).astype(BF16)


BLOCKS = ((0, 512), (512, 1024), (1536, 1024), (2560, 1024), (3584, 384), (3968, 128))
AHEAD = 3


def merge_kernel(
    grad, error, q, merged, left_t, factor, grad_v, error_v, q_v, sems, q_sem
):
    def copies(i):
        start, width = BLOCKS[i]
        columns = pl.ds(start, width)
        return (
            pltpu.make_async_copy(
                grad.at[:, columns], grad_v.at[:, columns], sems.at[0, i]
            ),
            pltpu.make_async_copy(
                error.at[:, columns], error_v.at[:, columns], sems.at[1, i]
            ),
        )

    q_copy = pltpu.make_async_copy(q, q_v, q_sem)
    q_copy.start()
    for i in range(AHEAD):
        for copy in copies(i):
            copy.start()
    left = None
    for i, (start, width) in enumerate(BLOCKS):
        for copy in copies(i):
            copy.wait()
        if i + AHEAD < len(BLOCKS):
            for copy in copies(i + AHEAD):
                copy.start()
        if i == 0:
            q_copy.wait()
            factor[...] = q_v[...].astype(BF16)
        columns = pl.ds(start, width)
        block = (grad_v[:, columns].astype(F32) + error_v[:, columns].astype(F32)).astype(BF16)
        merged[:, columns] = block
        term = lax.dot_general(
            factor[:, columns],
            block,
            (((1,), (1,)), ((), ())),
            preferred_element_type=F32,
        )
        left = term if left is None else left + term
    left_t[...] = left * 0.125


def merge(grad, error, q):
    hbm = pl.BlockSpec(memory_space=pltpu.HBM)
    vmem = pl.BlockSpec(memory_space=pltpu.VMEM)
    return pl.pallas_call(
        merge_kernel,
        out_shape=(
            pltpu.VMEM((ROWS, COLS), BF16),
            pltpu.VMEM((RANK, ROWS), F32),
            pltpu.VMEM((RANK, COLS), BF16),
        ),
        in_specs=[hbm] * 3,
        out_specs=(vmem, vmem, vmem),
        scratch_shapes=[
            pltpu.VMEM((ROWS, COLS), BF16),
            pltpu.VMEM((ROWS, COLS), BF16),
            pltpu.VMEM((RANK, COLS), F32),
            pltpu.SemaphoreType.DMA((2, len(BLOCKS))),
            pltpu.SemaphoreType.DMA,
        ],
        compiler_params=pltpu.CompilerParams(vmem_limit_bytes=LIMIT),
        name="merge_left",
    )(*(pltpu.with_memory_space_constraint(x, pltpu.HBM) for x in (grad, error, q)))


def turn_kernel(factor, factor_t):
    factor_t[...] = factor[...].T


def turned(factor):
    return pl.pallas_call(
        turn_kernel,
        out_shape=pltpu.VMEM((COLS, RANK), BF16),
        in_specs=[pl.BlockSpec(memory_space=pltpu.VMEM)],
        out_specs=pl.BlockSpec(memory_space=pltpu.VMEM),
        compiler_params=pltpu.CompilerParams(vmem_limit_bytes=LIMIT),
        cost_estimate=pl.CostEstimate(flops=0, bytes_accessed=1 << 20, transcendentals=0),
        name="turn_factor",
    )(factor)


def right_kernel(own, one, two, three, merged, after, left_t, parts):
    left = (own[...] + one[...]) + (two[...] + three[...])
    left_t[...] = left
    pieces = jnp.concatenate(split3(left), axis=0)
    for tile in range(0, COLS, 512):
        product = jnp.dot(
            pieces, merged[:, tile : tile + 512], preferred_element_type=F32
        )
        product = (product[2 * RANK :] + product[RANK : 2 * RANK]) + product[:RANK]
        for j in range(4):
            for g in range(GROUPS):
                parts[g * TILES + tile // LANES + j] = product[
                    g * GROUP : (g + 1) * GROUP, j * LANES : (j + 1) * LANES
                ]


def right_product(own, one, two, three, merged, after):
    return pl.pallas_call(
        right_kernel,
        out_shape=(
            pltpu.VMEM((RANK, ROWS), F32),
            pltpu.VMEM((GROUPS * TILES, GROUP, LANES), F32),
        ),
        in_specs=[pl.BlockSpec(memory_space=pltpu.VMEM)] * 5
        + [pl.BlockSpec(memory_space=pl.ANY)],
        out_specs=(pl.BlockSpec(memory_space=pltpu.VMEM),) * 2,
        compiler_params=pltpu.CompilerParams(vmem_limit_bytes=LIMIT),
        name="right_parts",
    )(own, one, two, three, pltpu.with_memory_space_constraint(merged, pltpu.VMEM), after)


def sum_kernel(parts, chunks):
    total = jnp.sum(parts[...], axis=0, keepdims=True)
    chunks[...] = jnp.broadcast_to(total, chunks.shape)


def sum_parts(parts):
    return pl.pallas_call(
        sum_kernel,
        out_shape=pltpu.VMEM(parts.shape, F32),
        in_specs=[pl.BlockSpec(memory_space=pltpu.VMEM)],
        out_specs=pl.BlockSpec(memory_space=pltpu.VMEM),
        compiler_params=pltpu.CompilerParams(vmem_limit_bytes=LIMIT),
        name="sum_parts",
    )(pltpu.with_memory_space_constraint(parts, pltpu.VMEM))


OWN = COLS // 8
OUT_STEPS = COLS // OWN


def inverse_factor(gram):
    width = 2 * RANK
    row = lax.broadcasted_iota(jnp.int32, (RANK, RANK), 0)
    col = lax.broadcasted_iota(jnp.int32, (RANK, RANK), 1)
    work = jnp.concatenate([gram, (row == col).astype(F32)], axis=1)
    rows_at = lax.broadcasted_iota(jnp.int32, (RANK, width), 0)
    columns = [jnp.broadcast_to(gram[:, k : k + 1], (RANK, width)) for k in range(RANK)]
    result = jnp.zeros((RANK, width), F32)
    for k in range(RANK):
        pivot = jnp.broadcast_to(columns[k][k : k + 1], (RANK, width))
        pivot_row = jnp.broadcast_to(work[k : k + 1], (RANK, width))
        result = jnp.where(rows_at == k, pivot_row * lax.rsqrt(pivot), result)
        ratio = jnp.where(rows_at > k, columns[k], 0.0) / pivot
        work = work - ratio * pivot_row
        for j in range(k + 1, RANK):
            columns[j] = columns[j] - ratio * columns[j][k : k + 1]
    return result[:, RANK:]


def stacked(left, right):
    a, b, c = split3(left)
    x, y, z = split3(right)
    return (
        jnp.concatenate([c, b, a, b, a, a], axis=1),
        jnp.concatenate([x, y, z, x, y, x], axis=0),
    )


def finish_kernel(
    parts, left_t, factor_t, merged, approx, new_error, right,
    total_v, right_v, right_b, approx_v, error_v, sems, approx_sem, right_sem,
):
    for j in range(TILES):
        for g in range(GROUPS):
            total_v[g * GROUP : (g + 1) * GROUP, j * LANES : (j + 1) * LANES] = (
                parts[g * TILES + j] * 0.125
            )
    gram = lax.dot_general(
        jnp.concatenate(split3(total_v[...]), axis=0),
        factor_t[...],
        (((1,), (0,)), ((), ())),
        preferred_element_type=F32,
    )
    gram = (gram[2 * RANK :] + gram[RANK : 2 * RANK]) + gram[:RANK]
    inverse = inverse_factor(gram)
    lhs, rhs = stacked(inverse, left_t[...])
    basis = jnp.dot(lhs, rhs, preferred_element_type=F32).astype(BF16).T
    place = lax.axis_index("dp")

    def error_copy(step):
        columns = pl.ds(pl.multiple_of(lax.rem(place + step, OUT_STEPS) * OWN, OWN), OWN)
        return pltpu.make_async_copy(
            error_v.at[:, columns], new_error.at[:, columns], sems.at[step]
        )

    approx_copy = pltpu.make_async_copy(approx_v, approx, approx_sem)
    right_copy = pltpu.make_async_copy(right_v, right, right_sem)
    lhs, rhs = stacked(inverse, total_v[...])
    total = jnp.dot(lhs, rhs, preferred_element_type=F32)
    right_v[...] = total
    right_copy.start()
    right_b[...] = total.astype(BF16)
    for step in range(OUT_STEPS):
        columns = pl.ds(pl.multiple_of(lax.rem(place + step, OUT_STEPS) * OWN, OWN), OWN)
        product = jnp.dot(basis, right_b[:, columns], preferred_element_type=F32)
        error_v[:, columns] = (merged[:, columns].astype(F32) - product).astype(BF16)
        error_copy(step).start()
        if step == 0:
            approx_v[...] = product.astype(BF16)
            approx_copy.start()
    for step in range(OUT_STEPS):
        error_copy(step).wait()
    approx_copy.wait()
    right_copy.wait()


def finish(parts, left_t, factor_t, merged):
    vmem = pl.BlockSpec(memory_space=pltpu.VMEM)
    hbm = pl.BlockSpec(memory_space=pltpu.HBM)
    return pl.pallas_call(
        finish_kernel,
        out_shape=(
            jax.ShapeDtypeStruct((ROWS, OWN), BF16),
            jax.ShapeDtypeStruct((ROWS, COLS), BF16),
            jax.ShapeDtypeStruct((RANK, COLS), F32),
        ),
        in_specs=[vmem] * 4,
        out_specs=(hbm, hbm, hbm),
        scratch_shapes=[
            pltpu.VMEM((RANK, COLS), F32),
            pltpu.VMEM((RANK, COLS), F32),
            pltpu.VMEM((RANK, COLS), BF16),
            pltpu.VMEM((ROWS, OWN), BF16),
            pltpu.VMEM((ROWS, COLS), BF16),
            pltpu.SemaphoreType.DMA((OUT_STEPS,)),
            pltpu.SemaphoreType.DMA,
            pltpu.SemaphoreType.DMA,
        ],
        compiler_params=pltpu.CompilerParams(vmem_limit_bytes=LIMIT),
        name="finish",
    )(parts, left_t, factor_t, pltpu.with_memory_space_constraint(merged, pltpu.VMEM))


def local(grad_attn, error_attn, q_attn):
    merged, left_t, factor = merge(grad_attn[0], error_attn[0], q_attn)
    factor_t = turned(factor)

    def moved(value, pairs):
        return lax.ppermute(value, "dp", pairs)

    pair = left_t + moved(left_t, [(i, i ^ 1) for i in range(8)])
    others = [moved(pair, [(i, i ^ (2 * k)) for i in range(8)]) for k in (1, 2, 3)]
    left_t, parts = right_product(pair, *others, merged, factor_t)
    parts = lax.all_to_all(parts, ("dp", "tensor"), 0, 0, tiled=True)
    parts = sum_parts(parts)
    parts = lax.all_to_all(parts, ("dp", "tensor"), 0, 0, tiled=True)
    approx, new_error, right = finish(parts, left_t, factor_t, merged)
    return (approx, new_error[None], right)


def solution(mesh):
    placed = (P("dp", "tensor", None), P("dp", "tensor", None), P())
    return jax.shard_map(
        local,
        mesh=mesh,
        in_specs=placed,
        out_specs=(P("tensor", "dp"), P("dp", "tensor", None), P()),
        check_vma=False,
    )
```

```python
import functools

import jax
import jax.numpy as jnp
from jax import lax
from jax.experimental import pallas as pl
from jax.experimental.pallas import tpu as pltpu
from jax.sharding import PartitionSpec as P

F32, BF16 = jnp.float32, jnp.bfloat16
ROWS, COLS, RANK = 512, 4096, 16
LANES = 128
TILES = COLS // LANES
GROUP = 4
GROUPS = RANK // GROUP
LIMIT = 40 * 1024 * 1024


def split3(value):
    high = value.astype(BF16)
    rest = value - high.astype(F32)
    middle = rest.astype(BF16)
    return high, middle, (rest - middle.astype(F32)).astype(BF16)


BLOCKS = ((0, 512), (512, 768), (1280, 1024), (2304, 1024), (3328, 512), (3840, 256))
AHEAD = 3


def merge_kernel(
    grad, error, q, merged, left_t, factor, grad_v, error_v, q_v, sems, q_sem
):
    def copies(i):
        start, width = BLOCKS[i]
        columns = pl.ds(start, width)
        return (
            pltpu.make_async_copy(
                grad.at[:, columns], grad_v.at[:, columns], sems.at[0, i]
            ),
            pltpu.make_async_copy(
                error.at[:, columns], error_v.at[:, columns], sems.at[1, i]
            ),
        )

    q_copy = pltpu.make_async_copy(q, q_v, q_sem)
    q_copy.start()
    for i in range(AHEAD):
        for copy in copies(i):
            copy.start()
    left = None
    for i, (start, width) in enumerate(BLOCKS):
        for copy in copies(i):
            copy.wait()
        if i + AHEAD < len(BLOCKS):
            for copy in copies(i + AHEAD):
                copy.start()
        if i == 0:
            q_copy.wait()
            factor[...] = q_v[...].astype(BF16)
        columns = pl.ds(start, width)
        block = (grad_v[:, columns].astype(F32) + error_v[:, columns].astype(F32)).astype(BF16)
        merged[:, columns] = block
        term = lax.dot_general(
            factor[:, columns],
            block,
            (((1,), (1,)), ((), ())),
            preferred_element_type=F32,
        )
        left = term if left is None else left + term
    left_t[...] = left * 0.125


def merge(grad, error, q):
    hbm = pl.BlockSpec(memory_space=pltpu.HBM)
    vmem = pl.BlockSpec(memory_space=pltpu.VMEM)
    return pl.pallas_call(
        merge_kernel,
        out_shape=(
            pltpu.VMEM((ROWS, COLS), BF16),
            pltpu.VMEM((RANK, ROWS), F32),
            pltpu.VMEM((RANK, COLS), BF16),
        ),
        in_specs=[hbm] * 3,
        out_specs=(vmem, vmem, vmem),
        scratch_shapes=[
            pltpu.VMEM((ROWS, COLS), BF16),
            pltpu.VMEM((ROWS, COLS), BF16),
            pltpu.VMEM((RANK, COLS), F32),
            pltpu.SemaphoreType.DMA((2, len(BLOCKS))),
            pltpu.SemaphoreType.DMA,
        ],
        compiler_params=pltpu.CompilerParams(vmem_limit_bytes=LIMIT),
        name="merge_left",
    )(*(pltpu.with_memory_space_constraint(x, pltpu.HBM) for x in (grad, error, q)))


def turn_kernel(factor, factor_t):
    factor_t[...] = factor[...].T


def turned(factor):
    return pl.pallas_call(
        turn_kernel,
        out_shape=pltpu.VMEM((COLS, RANK), BF16),
        in_specs=[pl.BlockSpec(memory_space=pltpu.VMEM)],
        out_specs=pl.BlockSpec(memory_space=pltpu.VMEM),
        compiler_params=pltpu.CompilerParams(vmem_limit_bytes=LIMIT),
        cost_estimate=pl.CostEstimate(flops=0, bytes_accessed=1 << 20, transcendentals=0),
        name="turn_factor",
    )(factor)


def right_kernel(own, one, two, three, merged, after, left_t, parts):
    left = (own[...] + one[...]) + (two[...] + three[...])
    left_t[...] = left
    pieces = jnp.concatenate(split3(left), axis=0)
    for tile in range(0, COLS, 512):
        product = jnp.dot(
            pieces, merged[:, tile : tile + 512], preferred_element_type=F32
        )
        product = (product[2 * RANK :] + product[RANK : 2 * RANK]) + product[:RANK]
        for j in range(4):
            for g in range(GROUPS):
                parts[g * TILES + tile // LANES + j] = product[
                    g * GROUP : (g + 1) * GROUP, j * LANES : (j + 1) * LANES
                ]


def right_product(own, one, two, three, merged, after):
    return pl.pallas_call(
        right_kernel,
        out_shape=(
            pltpu.VMEM((RANK, ROWS), F32),
            pltpu.VMEM((GROUPS * TILES, GROUP, LANES), F32),
        ),
        in_specs=[pl.BlockSpec(memory_space=pltpu.VMEM)] * 5
        + [pl.BlockSpec(memory_space=pl.ANY)],
        out_specs=(pl.BlockSpec(memory_space=pltpu.VMEM),) * 2,
        compiler_params=pltpu.CompilerParams(vmem_limit_bytes=LIMIT),
        name="right_parts",
    )(own, one, two, three, pltpu.with_memory_space_constraint(merged, pltpu.VMEM), after)


def sum_kernel(parts, chunks):
    total = jnp.sum(parts[...], axis=0, keepdims=True)
    chunks[...] = jnp.broadcast_to(total, chunks.shape)


def sum_parts(parts):
    return pl.pallas_call(
        sum_kernel,
        out_shape=pltpu.VMEM(parts.shape, F32),
        in_specs=[pl.BlockSpec(memory_space=pltpu.VMEM)],
        out_specs=pl.BlockSpec(memory_space=pltpu.VMEM),
        compiler_params=pltpu.CompilerParams(vmem_limit_bytes=LIMIT),
        name="sum_parts",
    )(pltpu.with_memory_space_constraint(parts, pltpu.VMEM))


OWN = COLS // 8
OUT_STEPS = COLS // OWN


def inverse_factor(gram):
    width = 2 * RANK
    row = lax.broadcasted_iota(jnp.int32, (RANK, RANK), 0)
    col = lax.broadcasted_iota(jnp.int32, (RANK, RANK), 1)
    work = jnp.concatenate([gram, (row == col).astype(F32)], axis=1)
    rows_at = lax.broadcasted_iota(jnp.int32, (RANK, width), 0)
    columns = [jnp.broadcast_to(gram[:, k : k + 1], (RANK, width)) for k in range(RANK)]
    result = jnp.zeros((RANK, width), F32)
    for k in range(RANK):
        pivot = jnp.broadcast_to(columns[k][k : k + 1], (RANK, width))
        pivot_row = jnp.broadcast_to(work[k : k + 1], (RANK, width))
        result = jnp.where(rows_at == k, pivot_row * lax.rsqrt(pivot), result)
        ratio = jnp.where(rows_at > k, columns[k], 0.0) / pivot
        work = work - ratio * pivot_row
        for j in range(k + 1, RANK):
            columns[j] = columns[j] - ratio * columns[j][k : k + 1]
    return result[:, RANK:]


def stacked(left, right):
    a, b, c = split3(left)
    x, y, z = split3(right)
    return (
        jnp.concatenate([c, b, a, b, a, a], axis=1),
        jnp.concatenate([x, y, z, x, y, x], axis=0),
    )


def finish_kernel(
    parts, left_t, factor_t, merged, approx, new_error, right,
    total_v, right_v, right_b, approx_v, error_v, sems, approx_sem, right_sem,
):
    for j in range(TILES):
        for g in range(GROUPS):
            total_v[g * GROUP : (g + 1) * GROUP, j * LANES : (j + 1) * LANES] = (
                parts[g * TILES + j] * 0.125
            )
    gram = lax.dot_general(
        jnp.concatenate(split3(total_v[...]), axis=0),
        factor_t[...],
        (((1,), (0,)), ((), ())),
        preferred_element_type=F32,
    )
    gram = (gram[2 * RANK :] + gram[RANK : 2 * RANK]) + gram[:RANK]
    inverse = inverse_factor(gram)
    lhs, rhs = stacked(inverse, left_t[...])
    basis = jnp.dot(lhs, rhs, preferred_element_type=F32).astype(BF16).T
    place = lax.axis_index("dp")

    def error_copy(step):
        columns = pl.ds(pl.multiple_of(lax.rem(place + step, OUT_STEPS) * OWN, OWN), OWN)
        return pltpu.make_async_copy(
            error_v.at[:, columns], new_error.at[:, columns], sems.at[step]
        )

    approx_copy = pltpu.make_async_copy(approx_v, approx, approx_sem)
    right_copy = pltpu.make_async_copy(right_v, right, right_sem)
    lhs, rhs = stacked(inverse, total_v[...])
    total = jnp.dot(lhs, rhs, preferred_element_type=F32)
    right_v[...] = total
    right_copy.start()
    right_b[...] = total.astype(BF16)
    for step in range(OUT_STEPS):
        columns = pl.ds(pl.multiple_of(lax.rem(place + step, OUT_STEPS) * OWN, OWN), OWN)
        product = jnp.dot(basis, right_b[:, columns], preferred_element_type=F32)
        error_v[:, columns] = (merged[:, columns].astype(F32) - product).astype(BF16)
        error_copy(step).start()
        if step == 0:
            approx_v[...] = product.astype(BF16)
            approx_copy.start()
    for step in range(OUT_STEPS):
        error_copy(step).wait()
    approx_copy.wait()
    right_copy.wait()


def finish(parts, left_t, factor_t, merged):
    vmem = pl.BlockSpec(memory_space=pltpu.VMEM)
    hbm = pl.BlockSpec(memory_space=pltpu.HBM)
    return pl.pallas_call(
        finish_kernel,
        out_shape=(
            jax.ShapeDtypeStruct((ROWS, OWN), BF16),
            jax.ShapeDtypeStruct((ROWS, COLS), BF16),
            jax.ShapeDtypeStruct((RANK, COLS), F32),
        ),
        in_specs=[vmem] * 4,
        out_specs=(hbm, hbm, hbm),
        scratch_shapes=[
            pltpu.VMEM((RANK, COLS), F32),
            pltpu.VMEM((RANK, COLS), F32),
            pltpu.VMEM((RANK, COLS), BF16),
            pltpu.VMEM((ROWS, OWN), BF16),
            pltpu.VMEM((ROWS, COLS), BF16),
            pltpu.SemaphoreType.DMA((OUT_STEPS,)),
            pltpu.SemaphoreType.DMA,
            pltpu.SemaphoreType.DMA,
        ],
        compiler_params=pltpu.CompilerParams(vmem_limit_bytes=LIMIT),
        name="finish",
    )(parts, left_t, factor_t, pltpu.with_memory_space_constraint(merged, pltpu.VMEM))


def local(grad_attn, error_attn, q_attn):
    merged, left_t, factor = merge(grad_attn[0], error_attn[0], q_attn)
    factor_t = turned(factor)

    def moved(value, pairs):
        return lax.ppermute(value, "dp", pairs)

    pair = left_t + moved(left_t, [(i, i ^ 1) for i in range(8)])
    others = [moved(pair, [(i, i ^ (2 * k)) for i in range(8)]) for k in (1, 2, 3)]
    left_t, parts = right_product(pair, *others, merged, factor_t)
    parts = lax.all_to_all(parts, ("dp", "tensor"), 0, 0, tiled=True)
    parts = sum_parts(parts)
    parts = lax.all_to_all(parts, ("dp", "tensor"), 0, 0, tiled=True)
    approx, new_error, right = finish(parts, left_t, factor_t, merged)
    return (approx, new_error[None], right)


def solution(mesh):
    placed = (P("dp", "tensor", None), P("dp", "tensor", None), P())
    return jax.shard_map(
        local,
        mesh=mesh,
        in_specs=placed,
        out_specs=(P("tensor", "dp"), P("dp", "tensor", None), P()),
        check_vma=False,
    )
```

```python
import functools

import jax
import jax.numpy as jnp
from jax import lax
from jax.experimental import pallas as pl
from jax.experimental.pallas import tpu as pltpu
from jax.sharding import PartitionSpec as P

F32, BF16 = jnp.float32, jnp.bfloat16
ROWS, COLS, RANK = 512, 4096, 16
LANES = 128
TILES = COLS // LANES
GROUP = 4
GROUPS = RANK // GROUP
LIMIT = 40 * 1024 * 1024


def split3(value):
    high = value.astype(BF16)
    rest = value - high.astype(F32)
    middle = rest.astype(BF16)
    return high, middle, (rest - middle.astype(F32)).astype(BF16)


BLOCKS = ((0, 256), (256, 768), (1024, 768), (1792, 1024), (2816, 768), (3584, 384), (3968, 128))
AHEAD = 3


def merge_kernel(
    grad, error, q, merged, left_t, factor, grad_v, error_v, q_v, sems, q_sem
):
    def copies(i):
        start, width = BLOCKS[i]
        columns = pl.ds(start, width)
        return (
            pltpu.make_async_copy(
                grad.at[:, columns], grad_v.at[:, columns], sems.at[0, i]
            ),
            pltpu.make_async_copy(
                error.at[:, columns], error_v.at[:, columns], sems.at[1, i]
            ),
        )

    q_copy = pltpu.make_async_copy(q, q_v, q_sem)
    q_copy.start()
    for i in range(AHEAD):
        for copy in copies(i):
            copy.start()
    left = None
    for i, (start, width) in enumerate(BLOCKS):
        for copy in copies(i):
            copy.wait()
        for later in (AHEAD, AHEAD + 1) if i == 0 else (i + AHEAD + 1,):
            if later < len(BLOCKS):
                for copy in copies(later):
                    copy.start()
        if i == 0:
            q_copy.wait()
            factor[...] = q_v[...].astype(BF16)
        columns = pl.ds(start, width)
        block = (grad_v[:, columns].astype(F32) + error_v[:, columns].astype(F32)).astype(BF16)
        merged[:, columns] = block
        term = lax.dot_general(
            factor[:, columns],
            block,
            (((1,), (1,)), ((), ())),
            preferred_element_type=F32,
        )
        left = term if left is None else left + term
    left_t[...] = left * 0.125


def merge(grad, error, q):
    hbm = pl.BlockSpec(memory_space=pltpu.HBM)
    vmem = pl.BlockSpec(memory_space=pltpu.VMEM)
    return pl.pallas_call(
        merge_kernel,
        out_shape=(
            pltpu.VMEM((ROWS, COLS), BF16),
            pltpu.VMEM((RANK, ROWS), F32),
            pltpu.VMEM((RANK, COLS), BF16),
        ),
        in_specs=[hbm] * 3,
        out_specs=(vmem, vmem, vmem),
        scratch_shapes=[
            pltpu.VMEM((ROWS, COLS), BF16),
            pltpu.VMEM((ROWS, COLS), BF16),
            pltpu.VMEM((RANK, COLS), F32),
            pltpu.SemaphoreType.DMA((2, len(BLOCKS))),
            pltpu.SemaphoreType.DMA,
        ],
        compiler_params=pltpu.CompilerParams(vmem_limit_bytes=LIMIT),
        name="merge_left",
    )(*(pltpu.with_memory_space_constraint(x, pltpu.HBM) for x in (grad, error, q)))


def turn_kernel(factor, factor_t):
    factor_t[...] = factor[...].T


def turned(factor):
    return pl.pallas_call(
        turn_kernel,
        out_shape=pltpu.VMEM((COLS, RANK), BF16),
        in_specs=[pl.BlockSpec(memory_space=pltpu.VMEM)],
        out_specs=pl.BlockSpec(memory_space=pltpu.VMEM),
        compiler_params=pltpu.CompilerParams(vmem_limit_bytes=LIMIT),
        cost_estimate=pl.CostEstimate(flops=0, bytes_accessed=1 << 20, transcendentals=0),
        name="turn_factor",
    )(factor)


def right_kernel(own, one, two, three, merged, after, left_t, parts):
    left = (own[...] + one[...]) + (two[...] + three[...])
    left_t[...] = left
    pieces = jnp.concatenate(split3(left), axis=0)
    for tile in range(0, COLS, 512):
        product = jnp.dot(
            pieces, merged[:, tile : tile + 512], preferred_element_type=F32
        )
        product = (product[2 * RANK :] + product[RANK : 2 * RANK]) + product[:RANK]
        for j in range(4):
            for g in range(GROUPS):
                parts[g * TILES + tile // LANES + j] = product[
                    g * GROUP : (g + 1) * GROUP, j * LANES : (j + 1) * LANES
                ]


def right_product(own, one, two, three, merged, after):
    return pl.pallas_call(
        right_kernel,
        out_shape=(
            pltpu.VMEM((RANK, ROWS), F32),
            pltpu.VMEM((GROUPS * TILES, GROUP, LANES), F32),
        ),
        in_specs=[pl.BlockSpec(memory_space=pltpu.VMEM)] * 5
        + [pl.BlockSpec(memory_space=pl.ANY)],
        out_specs=(pl.BlockSpec(memory_space=pltpu.VMEM),) * 2,
        compiler_params=pltpu.CompilerParams(vmem_limit_bytes=LIMIT),
        name="right_parts",
    )(own, one, two, three, pltpu.with_memory_space_constraint(merged, pltpu.VMEM), after)


def sum_kernel(parts, chunks):
    total = jnp.sum(parts[...], axis=0, keepdims=True)
    chunks[...] = jnp.broadcast_to(total, chunks.shape)


def sum_parts(parts):
    return pl.pallas_call(
        sum_kernel,
        out_shape=pltpu.VMEM(parts.shape, F32),
        in_specs=[pl.BlockSpec(memory_space=pltpu.VMEM)],
        out_specs=pl.BlockSpec(memory_space=pltpu.VMEM),
        compiler_params=pltpu.CompilerParams(vmem_limit_bytes=LIMIT),
        name="sum_parts",
    )(pltpu.with_memory_space_constraint(parts, pltpu.VMEM))


OWN = COLS // 8
OUT_STEPS = COLS // OWN


def inverse_factor(gram):
    width = 2 * RANK
    row = lax.broadcasted_iota(jnp.int32, (RANK, RANK), 0)
    col = lax.broadcasted_iota(jnp.int32, (RANK, RANK), 1)
    work = jnp.concatenate([gram, (row == col).astype(F32)], axis=1)
    rows_at = lax.broadcasted_iota(jnp.int32, (RANK, width), 0)
    columns = [jnp.broadcast_to(gram[:, k : k + 1], (RANK, width)) for k in range(RANK)]
    result = jnp.zeros((RANK, width), F32)
    for k in range(RANK):
        pivot = jnp.broadcast_to(columns[k][k : k + 1], (RANK, width))
        pivot_row = jnp.broadcast_to(work[k : k + 1], (RANK, width))
        result = jnp.where(rows_at == k, pivot_row * lax.rsqrt(pivot), result)
        ratio = jnp.where(rows_at > k, columns[k], 0.0) / pivot
        work = work - ratio * pivot_row
        for j in range(k + 1, RANK):
            columns[j] = columns[j] - ratio * columns[j][k : k + 1]
    return result[:, RANK:]


def stacked(left, right):
    a, b, c = split3(left)
    x, y, z = split3(right)
    return (
        jnp.concatenate([c, b, a, b, a, a], axis=1),
        jnp.concatenate([x, y, z, x, y, x], axis=0),
    )


def finish_kernel(
    parts, left_t, factor_t, merged, approx, new_error, right,
    total_v, right_v, right_b, approx_v, error_v, sems, approx_sem, right_sem,
):
    for j in range(TILES):
        for g in range(GROUPS):
            total_v[g * GROUP : (g + 1) * GROUP, j * LANES : (j + 1) * LANES] = (
                parts[g * TILES + j] * 0.125
            )
    gram = lax.dot_general(
        jnp.concatenate(split3(total_v[...]), axis=0),
        factor_t[...],
        (((1,), (0,)), ((), ())),
        preferred_element_type=F32,
    )
    gram = (gram[2 * RANK :] + gram[RANK : 2 * RANK]) + gram[:RANK]
    inverse = inverse_factor(gram)
    lhs, rhs = stacked(inverse, left_t[...])
    basis = jnp.dot(lhs, rhs, preferred_element_type=F32).astype(BF16).T
    place = lax.axis_index("dp")

    def error_copy(step):
        columns = pl.ds(pl.multiple_of(lax.rem(place + step, OUT_STEPS) * OWN, OWN), OWN)
        return pltpu.make_async_copy(
            error_v.at[:, columns], new_error.at[:, columns], sems.at[step]
        )

    approx_copy = pltpu.make_async_copy(approx_v, approx, approx_sem)
    right_copy = pltpu.make_async_copy(right_v, right, right_sem)
    lhs, rhs = stacked(inverse, total_v[...])
    total = jnp.dot(lhs, rhs, preferred_element_type=F32)
    right_v[...] = total
    right_copy.start()
    right_b[...] = total.astype(BF16)
    for step in range(OUT_STEPS):
        columns = pl.ds(pl.multiple_of(lax.rem(place + step, OUT_STEPS) * OWN, OWN), OWN)
        product = jnp.dot(basis, right_b[:, columns], preferred_element_type=F32)
        error_v[:, columns] = (merged[:, columns].astype(F32) - product).astype(BF16)
        error_copy(step).start()
        if step == 0:
            approx_v[...] = product.astype(BF16)
            approx_copy.start()
    for step in range(OUT_STEPS):
        error_copy(step).wait()
    approx_copy.wait()
    right_copy.wait()


def finish(parts, left_t, factor_t, merged):
    vmem = pl.BlockSpec(memory_space=pltpu.VMEM)
    hbm = pl.BlockSpec(memory_space=pltpu.HBM)
    return pl.pallas_call(
        finish_kernel,
        out_shape=(
            jax.ShapeDtypeStruct((ROWS, OWN), BF16),
            jax.ShapeDtypeStruct((ROWS, COLS), BF16),
            jax.ShapeDtypeStruct((RANK, COLS), F32),
        ),
        in_specs=[vmem] * 4,
        out_specs=(hbm, hbm, hbm),
        scratch_shapes=[
            pltpu.VMEM((RANK, COLS), F32),
            pltpu.VMEM((RANK, COLS), F32),
            pltpu.VMEM((RANK, COLS), BF16),
            pltpu.VMEM((ROWS, OWN), BF16),
            pltpu.VMEM((ROWS, COLS), BF16),
            pltpu.SemaphoreType.DMA((OUT_STEPS,)),
            pltpu.SemaphoreType.DMA,
            pltpu.SemaphoreType.DMA,
        ],
        compiler_params=pltpu.CompilerParams(vmem_limit_bytes=LIMIT),
        name="finish",
    )(parts, left_t, factor_t, pltpu.with_memory_space_constraint(merged, pltpu.VMEM))


def local(grad_attn, error_attn, q_attn):
    merged, left_t, factor = merge(grad_attn[0], error_attn[0], q_attn)
    factor_t = turned(factor)

    def moved(value, pairs):
        return lax.ppermute(value, "dp", pairs)

    pair = left_t + moved(left_t, [(i, i ^ 1) for i in range(8)])
    others = [moved(pair, [(i, i ^ (2 * k)) for i in range(8)]) for k in (1, 2, 3)]
    left_t, parts = right_product(pair, *others, merged, factor_t)
    parts = lax.all_to_all(parts, ("dp", "tensor"), 0, 0, tiled=True)
    parts = sum_parts(parts)
    parts = lax.all_to_all(parts, ("dp", "tensor"), 0, 0, tiled=True)
    approx, new_error, right = finish(parts, left_t, factor_t, merged)
    return (approx, new_error[None], right)


def solution(mesh):
    placed = (P("dp", "tensor", None), P("dp", "tensor", None), P())
    return jax.shard_map(
        local,
        mesh=mesh,
        in_specs=placed,
        out_specs=(P("tensor", "dp"), P("dp", "tensor", None), P()),
        check_vma=False,
    )
```
